32 devices in a mesh: group: 2 (over x), fsdp: 8 (over z, y), dp: 2 (over core).
Axes of the slice: x: 2, y: 2, z: 4, core: 2. Of those that a mesh axis runs over, the one named last changes fastest.
Arguments:
- hidden: bfloat16 [2048, 28672], P(('group', 'dp'), 'fsdp'), parts along dimension 0, may hold values from -6 to 6
- cotangent: bfloat16 [2048, 8192], P(('group', 'dp'), 'fsdp'), parts along dimension 0, may hold values from -6 to 6
- down_weight: bfloat16 [28672, 8192], P('fsdp', 'dp'), may hold values from -0.0625 to 0.0625
- proj_in: bfloat16 [28672, 128], P('fsdp'), may hold values from -0.03125 to 0.03125
- proj_out: bfloat16 [8192, 64], replicated, may hold values from -0.0625 to 0.0625
- valid_proj: bfloat16 [2048, 8192], P(('group', 'fsdp')), parts along dimension 0, may hold values from -0.00390625 to 0.00390625
- lengths: int32 [8], P(('group', 'dp')), parts along dimension 0, may hold values from 64 to 256
Outputs:
- hidden_grad: bfloat16 [2048, 28672], P(('group', 'dp'), 'fsdp'), parts along dimension 0
- scores: float32 [8, 1024], P(('group', 'dp'), 'fsdp'), parts along dimension 0
The draws below stay inside these ranges and needn't reach their ends.
There are 2 independent parts, one for each index of `group`. The reference program is written for one: setup_inputs(seed, part) draws one part's arguments, and reference() takes and returns one part's arrays. A program takes and returns all parts, laid end to end along the dimension named above; an argument that names none is the same for every part. Nothing has to cross between parts.
All inputs are finite; a program needn't handle non-finite values.
Results may differ from the reference program's by a relative error of at most 0.0029.
Values may be sent and summed in bfloat16 or wider, within the bound.
A program may use at most 256 MiB of HBM per device.

```python
import jax
import jax.numpy as jnp
from jax import lax

D = 8192
FF = 28672
K_IN = 128
K_OUT = 64
SEQ = 256
VAL = 1024
EXAMPLES = 4
TOKENS = 1024


def place_ends(entries, rng, smallest, top_value):
    place = [jax.random.randint(jax.random.fold_in(rng, axis), (), 0, length) for axis, length in enumerate(entries.shape)]
    widest = entries.shape.index(max(entries.shape))
    beside = place[:widest] + [(place[widest] + 1) % entries.shape[widest]] + place[widest + 1:]
    return entries.at[tuple(place)].set(smallest).at[tuple(beside)].set(top_value)


def levels(rng, dims, split, low, largest):
    loudness, own = 1.0, jax.random.fold_in(rng, 6)
    for position, shards_of in split:
        steps = jnp.exp(jax.random.uniform(jax.random.fold_in(own, position), (shards_of,), jnp.float32, low / len(split), largest / len(split)))
        loudness = loudness * jnp.repeat(steps, dims[position] // shards_of).reshape([-1 if axis == position else 1 for axis in range(len(dims))])
    return loudness


def bell_draw(rng, shape, scale, bound, shards=(), held_as=jnp.bfloat16):
    drawn = jax.random.normal(rng, shape, jnp.float32) * scale
    if len(shards) > 0:
        drawn = levels(rng, shape, shards, -0.22, 0.18) * drawn
    return jnp.clip(drawn, min=-bound, max=bound).astype(held_as)


def setup_inputs(seed: int = 0, part: int = 0) -> dict:
    seeds = jax.random.split(jax.random.key(seed), 8)
    part_splits = jax.random.split(jax.random.fold_in(seeds[7], part), 8)
    return {
        "hidden": bell_draw(part_splits[0], (TOKENS, FF), 1.0, 6.0, ((0, 2), (1, 8))),
        "cotangent": bell_draw(part_splits[1], (TOKENS, D), 1.0, 6.0, ((0, 2), (1, 8))),
        "down_weight": bell_draw(seeds[2], (FF, D), D ** -0.5, 0.0625, ((0, 8), (1, 2))),
        "proj_in": bell_draw(seeds[3], (FF, K_IN), FF ** -0.5, 0.03125, ((0, 8),)),
        "proj_out": bell_draw(seeds[4], (D, K_OUT), D ** -0.5, 0.0625),
        "valid_proj": bell_draw(part_splits[5], (VAL, K_OUT * K_IN), (K_OUT * K_IN * SEQ) ** -0.5, 0.00390625, ((0, 8),)),
        "lengths": place_ends(jax.random.randint(part_splits[6], (EXAMPLES,), SEQ // 4, SEQ + 1), jax.random.fold_in(part_splits[6], 1), SEQ // 4, SEQ).astype(jnp.int32),
    }


def reference(hidden, cotangent, down_weight, proj_in, proj_out, valid_proj, lengths):
    positions = jnp.arange(SEQ, dtype=jnp.int32)
    keep_mask = (positions[None, :] < lengths[:, None]).astype(jnp.bfloat16).reshape(-1, 1)
    masked = cotangent * keep_mask
    hidden_grad = jnp.dot(masked, down_weight.T, preferred_element_type=jnp.float32).astype(jnp.bfloat16)
    acts = jnp.dot(hidden, proj_in, preferred_element_type=jnp.float32)
    outs = jnp.dot(masked, proj_out, preferred_element_type=jnp.float32)
    count = acts.shape[0] // SEQ
    grads = jnp.einsum("etk,etj->ekj", outs.reshape(count, SEQ, K_OUT), acts.reshape(count, SEQ, K_IN), precision=lax.Precision.HIGHEST)
    grads_low = grads.reshape(count, K_OUT * K_IN).astype(jnp.bfloat16)
    scores = jnp.dot(grads_low, valid_proj.T, preferred_element_type=jnp.float32)
    return hidden_grad, scores
```

```python
import functools

import jax
import jax.numpy as jnp
from jax import lax
from jax.experimental import pallas as pl
from jax.experimental.pallas import tpu as pltpu
from jax.sharding import PartitionSpec as P

K_IN = 128
K_OUT = 64
SEQ = 256
TILES = 7
ROWS = 128


def kernel(
    F, snake,
    len_ref, hid, cot, w, pin, pout, out, grads,
    X, W, acc, inc, stage, own, po, pi, part, rA, gR,
    ld_sem, w_sem, sib_send, sib_recv, ring_send, ring_recv,
    rs_send, rs_recv, gs_send, gs_recv, ex_send, ex_recv, out_sem,
):
    f = lax.axis_index("fsdp")
    c = lax.axis_index("dp")
    H = F // 2
    T, Dl = own.shape
    FFl = acc.shape[2]
    Tc = T // F
    tile = FFl // TILES

    if snake:
        y, z = lax.rem(f, 2), f // 2
        p = (1 - y) * z + y * (F - 1 - z)

        def at(q):
            h = q // H
            return (1 - h) * (2 * q) + h * (2 * F - 1 - 2 * q)
    else:
        p = f

        def at(q):
            return q

    targets = (at(lax.rem(p + 1, F)), at(lax.rem(p + F - 1, F)))

    def source(d, s):
        q = lax.rem(p - s + F, F) if d == 0 else lax.rem(p + s, F)
        src = at(q)
        half = src // H
        return src - half * H, 1 - (half + c - 2 * half * c)

    def rows(k):
        return pl.ds(k * SEQ, SEQ)

    def ring(slot, d, k):
        i = slot * 4 + d * 2 + k
        return pltpu.make_async_remote_copy(
            src_ref=X.at[slot, d, rows(k)],
            dst_ref=X.at[slot, d, rows(k)],
            send_sem=ring_send.at[i],
            recv_sem=ring_recv.at[i],
            device_id={"fsdp": targets[d]},
            device_id_type=pl.DeviceIdType.MESH,
        )

    def exchange(d, k):
        return pltpu.make_async_remote_copy(
            src_ref=acc.at[d, rows(k)],
            dst_ref=inc.at[rows(k)],
            send_sem=ex_send.at[k],
            recv_sem=ex_recv.at[k],
            device_id={"dp": 1 - c},
            device_id_type=pl.DeviceIdType.MESH,
        )

    my_half = f // H
    my_slot = f - my_half * H

    def sibling(d, k):
        return pltpu.make_async_remote_copy(
            src_ref=own.at[rows(k)],
            dst_ref=X.at[my_slot, d, rows(k)],
            send_sem=sib_send.at[k],
            recv_sem=sib_recv.at[k],
            device_id={"dp": 1 - c},
            device_id_type=pl.DeviceIdType.MESH,
        )

    load_cot = pltpu.make_async_copy(cot, own, ld_sem.at[0])
    load_cot.start()
    load_po = pltpu.make_async_copy(pout.at[pl.ds(f * Dl, Dl)], po, ld_sem.at[1])
    load_po.start()
    load_pi = pltpu.make_async_copy(pin, pi, ld_sem.at[2])
    load_pi.start()

    def load_hid(h):
        return pltpu.make_async_copy(
            hid.at[pl.ds(h * ROWS, ROWS)], stage.at[h % 2], ld_sem.at[3 + h % 2]
        )

    load_hid(0).start()
    load_hid(1).start()

    def load_w(i):
        return pltpu.make_async_copy(w.at[:, pl.ds(i * Dl, Dl)], W.at[i], w_sem.at[i])

    for i in range(H):
        load_w(i).start()

    barrier = pltpu.get_barrier_semaphore()

    @pl.loop(1, F)
    def _(j):
        pl.semaphore_signal(
            barrier, inc=1, device_id={"fsdp": lax.rem(f + j, F)},
            device_id_type=pl.DeviceIdType.MESH,
        )

    pl.semaphore_signal(
        barrier, inc=1, device_id={"dp": 1 - c}, device_id_type=pl.DeviceIdType.MESH
    )

    load_cot.wait()
    mine = my_half == c
    for k in range(2):
        position = lax.broadcasted_iota(jnp.int32, (SEQ, Dl), 0)
        block = own[rows(k), :]
        masked = jnp.where(position < len_ref[k], block.astype(jnp.float32), 0.0)
        own[rows(k), :] = masked.astype(block.dtype)
    pl.semaphore_wait(barrier, F)

    slot0, act0 = my_slot, 1 - (my_half + c - 2 * my_half * c)

    @pl.when(my_half != c)
    def _():
        for k in range(2):
            for d in range(2):
                @pl.when(c == d)
                def _():
                    sibling(d, k).start()

    @pl.when(mine)
    def _():
        for k in range(2):
            X[my_slot, c, rows(k), :] = own[rows(k), :]
        for d in range(2):
            @pl.when(c == d)
            def _():
                for k in range(2):
                    ring(my_slot, d, k).start()
        for d in range(2):
            @pl.when(c != d)
            def _():
                for k in range(2):
                    sibling(d, k).wait_recv()
                    ring(my_slot, d, k).start()

    load_po.wait()
    for k in range(2):
        o = jnp.dot(own[rows(k), :], po[...], preferred_element_type=jnp.float32)
        for j in range(SEQ // Tc):
            first = o[j * Tc : j * Tc + Tc // 2]
            second = o[j * Tc + Tc // 2 : (j + 1) * Tc]
            part[k * (SEQ // Tc) + j, Tc : Tc + Tc // 2, 0:K_OUT] = first
            part[k * (SEQ // Tc) + j, Tc : Tc + Tc // 2, K_OUT : 2 * K_OUT] = second
    load_pi.wait()
    for h in range(T // ROWS):
        load_hid(h).wait()
        a = jnp.dot(stage[h % 2], pi[...], preferred_element_type=jnp.float32)
        if h + 2 < T // ROWS:
            load_hid(h + 2).start()
        for j in range(ROWS // Tc):
            part[h * (ROWS // Tc) + j, 0:Tc, :] = a[j * Tc : (j + 1) * Tc]

    def scatter(t, src, dst):
        return pltpu.make_async_remote_copy(
            src_ref=part.at[src], dst_ref=rA.at[dst],
            send_sem=rs_send.at[t], recv_sem=rs_recv.at[dst],
            device_id={"fsdp": t}, device_id_type=pl.DeviceIdType.MESH,
        )

    def spread(t, dst):
        return pltpu.make_async_remote_copy(
            src_ref=gR.at[f], dst_ref=gR.at[dst],
            send_sem=gs_send.at[t], recv_sem=gs_recv.at[dst],
            device_id={"fsdp": t}, device_id_type=pl.DeviceIdType.MESH,
        )

    @pl.loop(1, F)
    def _(j):
        t = lax.rem(f + j, F)
        scatter(t, t, f).start()

    def reduce_acts():
        def add(j, total):
            t = lax.rem(f + j, F)
            scatter(t, t, t).wait_recv()
            return total + rA[t]

        total = lax.fori_loop(1, F, add, part[f])
        tn = (((0,), (0,)), ((), ()))
        g = jnp.zeros((K_OUT, K_IN), jnp.float32)
        for u in range(2):
            g = g + lax.dot_general(
                total[Tc : Tc + Tc // 2, u * K_OUT : (u + 1) * K_OUT],
                total[u * (Tc // 2) : (u + 1) * (Tc // 2), :],
                tn, precision=lax.Precision.HIGHEST,
                preferred_element_type=jnp.float32,
            )
        gR[f] = g

        @pl.loop(1, F)
        def _(j):
            t = lax.rem(f + j, F)
            spread(t, f).start()

    def reduce_grads():
        @pl.loop(1, F)
        def _(j):
            t = lax.rem(f + j, F)
            spread(t, t).wait_recv()

        for e in range(2):
            g = gR[e * H]
            for t in range(1, H):
                g = g + gR[e * H + t]
            grads[e] = g.astype(grads.dtype)

    def product(slot, d, k):
        block = X.at[slot, d, rows(k)]

        @pl.loop(0, TILES)
        def _(i):
            n = pl.ds(pl.multiple_of(i * tile, tile), tile)
            acc[d, rows(k), n] += lax.dot_general(
                block[...], W[slot, n, :], (((1,), (1,)), ((), ())),
                preferred_element_type=jnp.float32,
            )

    @pl.loop(0, T // 8)
    def _(i):
        r = pl.ds(pl.multiple_of(i * 8, 8), 8)
        for d in range(2):
            acc[d, r, :] = jnp.zeros((8, FFl), jnp.float32)

    for i in range(H):
        load_w(i).wait()

    @pl.when(mine)
    def _():
        for k in range(2):
            for d in range(2):
                product(my_slot, d, k)

    def step(s, counts):
        slots, acts, seen = [], [], []
        for d in range(2):
            slot, act = source(d, s)
            slots.append(slot)
            acts.append(act)
            seen.append(counts[d] + act)
        for k in range(2):
            for d in range(2):
                @pl.when(acts[d] == 1)
                def _():
                    ring(slots[d], d, k).wait_recv()

                    @pl.when(s < F - 1)
                    def _():
                        ring(slots[d], d, k).start()

            for d in range(2):
                @pl.when(acts[d] == 1)
                def _():
                    product(slots[d], d, k)

                    @pl.when(seen[d] == H)
                    def _():
                        @pl.when(c != d)
                        def _():
                            exchange(d, k).start()

        @pl.when(s == 3)
        def _():
            reduce_acts()

        @pl.when(s == 5)
        def _():
            reduce_grads()

        return tuple(seen)

    lax.fori_loop(1, F, step, (act0, act0))

    def write(b):
        return pltpu.make_async_copy(
            stage.at[b % 2], out.at[pl.ds(b * ROWS, ROWS)], out_sem.at[b % 2]
        )

    per = SEQ // ROWS
    for b in range(T // ROWS):
        if b % per == 0:
            exchange(0, b // per).wait_recv()
        if b >= 2:
            write(b - 2).wait()

        @pl.loop(0, ROWS // 16)
        def _(i):
            r = pl.ds(pl.multiple_of(b * ROWS + i * 16, 16), 16)
            o = pl.ds(pl.multiple_of(i * 16, 16), 16)
            stage[b % 2, o, :] = (acc[c, r, :] + inc[r, :]).astype(stage.dtype)

        write(b).start()

    for b in range(T // ROWS - 2, T // ROWS):
        write(b).wait()

    @pl.when(my_half != c)
    def _():
        for k in range(2):
            sibling(0, k).wait_send()

    for k in range(2):
        exchange(0, k).wait_send()

    @pl.loop(1, F)
    def _(j):
        t = lax.rem(f + j, F)
        scatter(t, t, f).wait_send()
        spread(t, f).wait_send()

    @pl.loop(0, F - 1)
    def _(s):
        for d in range(2):
            slot, act = source(d, s)

            @pl.when(act == 1)
            def _():
                for k in range(2):
                    ring(slot, d, k).wait_send()


def per_device(F, hidden, cotangent, down_weight, proj_in, proj_out, valid_proj, lengths):
    T, FFl = hidden.shape
    Dl = cotangent.shape[1]
    H = F // 2
    Tc = T // F
    any_spec = pl.BlockSpec(memory_space=pl.ANY)
    vmem = pl.BlockSpec(memory_space=pltpu.VMEM)
    dma = pltpu.SemaphoreType.DMA
    hidden_grad, grads_low = pl.pallas_call(
        functools.partial(kernel, F, F == 8),
        out_shape=(
            jax.ShapeDtypeStruct((T, FFl), jnp.bfloat16),
            jax.ShapeDtypeStruct((2, K_OUT, K_IN), jnp.bfloat16),
        ),
        in_specs=[pl.BlockSpec(memory_space=pltpu.SMEM)] + [any_spec] * 5,
        out_specs=(any_spec, vmem),
        scratch_shapes=[
            pltpu.VMEM((H, 2, T, Dl), jnp.bfloat16),
            pltpu.VMEM((H, FFl, Dl), jnp.bfloat16),
            pltpu.VMEM((2, T, FFl), jnp.float32),
            pltpu.VMEM((T, FFl), jnp.float32),
            pltpu.VMEM((2, ROWS, FFl), jnp.bfloat16),
            pltpu.VMEM((T, Dl), jnp.bfloat16),
            pltpu.VMEM((Dl, K_OUT), jnp.bfloat16),
            pltpu.VMEM((FFl, K_IN), jnp.bfloat16),
            pltpu.VMEM((F, Tc + Tc // 2, K_IN), jnp.float32),
            pltpu.VMEM((F, Tc + Tc // 2, K_IN), jnp.float32),
            pltpu.VMEM((F, K_OUT, K_IN), jnp.float32),
            dma((5,)), dma((H,)), dma((2,)), dma((2,)), dma((4 * H,)), dma((4 * H,)),
            dma((F,)), dma((F,)), dma((F,)), dma((F,)), dma((2,)), dma((2,)), dma((2,)),
        ],
        compiler_params=pltpu.CompilerParams(
            collective_id=0, has_side_effects=True, vmem_limit_bytes=66584576
        ),
    )(lengths, hidden, cotangent, down_weight, proj_in, proj_out)
    scores = lax.dot_general(
        grads_low.reshape(2, K_OUT * K_IN), valid_proj, (((1,), (1,)), ((), ())),
        preferred_element_type=jnp.float32,
    )
    return hidden_grad, scores


def solution(mesh):
    in_specs = (
        P(("group", "dp"), "fsdp"),
        P(("group", "dp"), "fsdp"),
        P("fsdp", "dp"),
        P("fsdp", None),
        P(),
        P(("group", "fsdp"), None),
        P(("group", "dp")),
    )
    out_specs = (P(("group", "dp"), "fsdp"), P(("group", "dp"), "fsdp"))
    return jax.shard_map(
        functools.partial(per_device, mesh.shape["fsdp"]),
        mesh=mesh, in_specs=in_specs, out_specs=out_specs, check_vma=False,
    )
```

```python
import functools

import jax
import jax.numpy as jnp
from jax import lax
from jax.experimental import pallas as pl
from jax.experimental.pallas import tpu as pltpu
from jax.sharding import PartitionSpec as P

K_IN = 128
K_OUT = 64
SEQ = 256
TILES = 7
CHUNK = 1024


def kernel(
    F, snake,
    len_ref, hid, cot, w, pin, pout, vp, out, scores,
    X, W, acc, inc, stage, own, po, pi, act, part, rA, gR, G, vbuf,
    ld_sem, w_sem, sib_send, sib_recv, ring_send, ring_recv,
    rs_send, rs_recv, gs_send, gs_recv, ex_send, ex_recv, out_sem, vp_sem,
):
    f = lax.axis_index("fsdp")
    c = lax.axis_index("dp")
    H = F // 2
    T, Dl = own.shape
    FFl = acc.shape[2]
    Tc = T // F
    tile = FFl // TILES

    if snake:
        y, z = lax.rem(f, 2), f // 2
        p = (1 - y) * z + y * (F - 1 - z)

        def at(q):
            h = q // H
            return (1 - h) * (2 * q) + h * (2 * F - 1 - 2 * q)
    else:
        p = f

        def at(q):
            return q

    targets = (at(lax.rem(p + 1, F)), at(lax.rem(p + F - 1, F)))

    def source(d, s):
        q = lax.rem(p - s + F, F) if d == 0 else lax.rem(p + s, F)
        src = at(q)
        half = src // H
        return src - half * H, 1 - (half + c - 2 * half * c)

    def rows(k):
        return pl.ds(k * SEQ, SEQ)

    def ring(slot, d, k):
        i = slot * 4 + d * 2 + k
        return pltpu.make_async_remote_copy(
            src_ref=X.at[slot, d, rows(k)],
            dst_ref=X.at[slot, d, rows(k)],
            send_sem=ring_send.at[i],
            recv_sem=ring_recv.at[i],
            device_id={"fsdp": targets[d]},
            device_id_type=pl.DeviceIdType.MESH,
        )

    def columns(i):
        return pl.ds(pl.multiple_of(i * tile, tile), tile)

    def exchange(d, i):
        return pltpu.make_async_remote_copy(
            src_ref=acc.at[d, :, columns(i)],
            dst_ref=inc.at[:, columns(i)],
            send_sem=ex_send.at[i],
            recv_sem=ex_recv.at[i],
            device_id={"dp": 1 - c},
            device_id_type=pl.DeviceIdType.MESH,
        )

    my_half = f // H
    my_slot = f - my_half * H

    def sibling(d, k):
        return pltpu.make_async_remote_copy(
            src_ref=own.at[rows(k)],
            dst_ref=X.at[my_slot, d, rows(k)],
            send_sem=sib_send.at[k],
            recv_sem=sib_recv.at[k],
            device_id={"dp": 1 - c},
            device_id_type=pl.DeviceIdType.MESH,
        )

    load_cot = pltpu.make_async_copy(cot, own, ld_sem.at[0])
    load_cot.start()
    load_po = pltpu.make_async_copy(
        pout.at[:, pl.ds(pl.multiple_of(f * Dl, Dl), Dl)], po, ld_sem.at[1]
    )
    load_po.start()
    load_pi = pltpu.make_async_copy(pin, pi, ld_sem.at[2])
    load_pi.start()

    def load_hid(h):
        return pltpu.make_async_copy(
            hid.at[:, pl.ds(h * tile, tile)], stage.at[h % 2], ld_sem.at[3 + h % 2]
        )

    load_hid(0).start()
    load_hid(1).start()

    def load_w(i):
        return pltpu.make_async_copy(w.at[:, pl.ds(i * Dl, Dl)], W.at[i], w_sem.at[i])

    def load_vp(q):
        return pltpu.make_async_copy(
            vp.at[:, pl.ds(q * CHUNK, CHUNK)], vbuf.at[q % 2], vp_sem.at[q % 2]
        )

    barrier = pltpu.get_barrier_semaphore()

    @pl.loop(1, F)
    def _(j):
        pl.semaphore_signal(
            barrier, inc=1, device_id={"fsdp": lax.rem(f + j, F)},
            device_id_type=pl.DeviceIdType.MESH,
        )

    pl.semaphore_signal(
        barrier, inc=1, device_id={"dp": 1 - c}, device_id_type=pl.DeviceIdType.MESH
    )

    load_cot.wait()
    for i in range(H):
        load_w(i).start()
    mine = my_half == c
    for k in range(2):
        position = lax.broadcasted_iota(jnp.int32, (SEQ, Dl), 0)
        block = own[rows(k), :]
        masked = jnp.where(position < len_ref[k], block.astype(jnp.float32), 0.0)
        own[rows(k), :] = masked.astype(block.dtype)
    pl.semaphore_wait(barrier, F)

    @pl.when(my_half != c)
    def _():
        for k in range(2):
            for d in range(2):
                @pl.when(c == d)
                def _():
                    sibling(d, k).start()

    @pl.when(mine)
    def _():
        for k in range(2):
            X[my_slot, c, rows(k), :] = own[rows(k), :]
        for d in range(2):
            @pl.when(c == d)
            def _():
                for k in range(2):
                    ring(my_slot, d, k).start()
        for d in range(2):
            @pl.when(c != d)
            def _():
                for k in range(2):
                    sibling(d, k).wait_recv()
                    ring(my_slot, d, k).start()

    @pl.loop(0, T // 8)
    def _(i):
        r = pl.ds(pl.multiple_of(i * 8, 8), 8)
        for d in range(2):
            acc[d, r, :] = jnp.zeros((8, FFl), jnp.float32)

    def project_out():
        load_po.wait()
        for k in range(2):
            o = lax.dot_general(
                own[rows(k), :], po[...], (((1,), (1,)), ((), ())),
                preferred_element_type=jnp.float32,
            )
            for j in range(SEQ // Tc):
                first = o[j * Tc : j * Tc + Tc // 2]
                second = o[j * Tc + Tc // 2 : (j + 1) * Tc]
                run = k * (SEQ // Tc) + j
                part[run, Tc : Tc + Tc // 2, 0:K_OUT] = first
                part[run, Tc : Tc + Tc // 2, K_OUT : 2 * K_OUT] = second

    def project_in(start, stop):
        for h in range(start, stop):
            load_hid(h).wait()
            a = jnp.dot(
                stage[h % 2], pi[h * tile : (h + 1) * tile, :],
                preferred_element_type=jnp.float32,
            )
            act[...] = a if h == 0 else act[...] + a
            if h + 2 < TILES:
                load_hid(h + 2).start()

    def scatter(t, src, dst):
        return pltpu.make_async_remote_copy(
            src_ref=part.at[src], dst_ref=rA.at[dst],
            send_sem=rs_send.at[t], recv_sem=rs_recv.at[dst],
            device_id={"fsdp": t}, device_id_type=pl.DeviceIdType.MESH,
        )

    def spread(t, dst):
        return pltpu.make_async_remote_copy(
            src_ref=gR.at[f], dst_ref=gR.at[dst],
            send_sem=gs_send.at[t], recv_sem=gs_recv.at[dst],
            device_id={"fsdp": t}, device_id_type=pl.DeviceIdType.MESH,
        )

    def scatter_acts():
        for j in range(F):
            part[j, 0:Tc, :] = act[j * Tc : (j + 1) * Tc, :]
        for q in range(2):
            load_vp(q).start()

        @pl.loop(1, F)
        def _(j):
            t = lax.rem(f + j, F)
            scatter(t, t, f).start()

    def reduce_acts():
        def add(j, total):
            t = lax.rem(f + j, F)
            scatter(t, t, t).wait_recv()
            return total + rA[t]

        total = lax.fori_loop(1, F, add, part[f])
        tn = (((0,), (0,)), ((), ()))
        g = jnp.zeros((K_OUT, K_IN), jnp.float32)
        for u in range(2):
            g = g + lax.dot_general(
                total[Tc : Tc + Tc // 2, u * K_OUT : (u + 1) * K_OUT],
                total[u * (Tc // 2) : (u + 1) * (Tc // 2), :],
                tn, precision=lax.Precision.HIGHEST,
                preferred_element_type=jnp.float32,
            )
        gR[f] = g

        @pl.loop(1, F)
        def _(j):
            t = lax.rem(f + j, F)
            spread(t, f).start()

    def reduce_grads():
        @pl.loop(1, F)
        def _(j):
            t = lax.rem(f + j, F)
            spread(t, t).wait_recv()

        for e in range(2):
            g = gR[e * H]
            for t in range(1, H):
                g = g + gR[e * H + t]
            G[e] = g
        total = jnp.zeros(scores.shape, jnp.float32)
        for q in range(K_OUT * K_IN // CHUNK):
            load_vp(q).wait()
            per = CHUNK // K_IN
            low = jnp.concatenate(
                [G[:, q * per + u, :] for u in range(per)], axis=1
            ).astype(jnp.bfloat16)
            total = total + lax.dot_general(
                low, vbuf[q % 2], (((1,), (1,)), ((), ())),
                preferred_element_type=jnp.float32,
            )
            if q + 2 < K_OUT * K_IN // CHUNK:
                load_vp(q + 2).start()
        scores[...] = total

    def product(slot, d, last):
        @pl.loop(0, TILES)
        def _(i):
            n = columns(i)
            acc[d, :, n] += lax.dot_general(
                X[slot, d], W[slot, n, :], (((1,), (1,)), ((), ())),
                preferred_element_type=jnp.float32,
            )

            @pl.when((last == 1) & (c != d))
            def _():
                exchange(d, i).start()

    def forward(s, d, k):
        slot, live = source(d, s)

        @pl.when(live == 1)
        def _():
            ring(slot, d, k).wait_recv()

            @pl.when(s < F - 1)
            def _():
                ring(slot, d, k).start()

    def final(count):
        return 1 - jnp.minimum(H - count, 1)

    def step(s, seen):
        counts = []
        for d in range(2):
            for e in range(2):
                forward(s, e, d)

            if d == 0:
                @pl.when(s == 1)
                def _():
                    load_pi.wait()
                    project_out()
                    project_in(0, 3)

                @pl.when(s == 2)
                def _():
                    for i in range(H):
                        load_w(i).wait()
            else:
                @pl.when(s == 1)
                def _():
                    project_in(3, TILES)
                    scatter_acts()

            @pl.when((s == 2) & mine)
            def _():
                product(my_slot, d, 0)

            slot, live = source(d, s - 1)
            counts.append(seen[d] + live)

            @pl.when((live == 1) & (s >= 2))
            def _():
                product(slot, d, final(counts[d]))

        @pl.when(s == 4)
        def _():
            reduce_acts()

        @pl.when(s == 6)
        def _():
            reduce_grads()

        return tuple(counts)

    seen = lax.fori_loop(1, F, step, (0, 0))
    for other in (True, False):
        for d in range(2):
            slot, live = source(d, F - 1)

            @pl.when((live == 1) & ((c != d) if other else (c == d)))
            def _():
                product(slot, d, final(seen[d] + live))

    def write(b):
        return pltpu.make_async_copy(
            stage.at[b % 2], out.at[:, pl.ds(b * tile, tile)], out_sem.at[b % 2]
        )

    for b in range(TILES):
        exchange(0, b).wait_recv()
        if b >= 2:
            write(b - 2).wait()

        @pl.loop(0, T // 16)
        def _(i):
            r = pl.ds(pl.multiple_of(i * 16, 16), 16)
            n = slice(b * tile, (b + 1) * tile)
            stage[b % 2, r, :] = (acc[c, r, n] + inc[r, n]).astype(stage.dtype)

        write(b).start()

    for b in range(TILES - 2, TILES):
        write(b).wait()

    @pl.when(my_half != c)
    def _():
        for k in range(2):
            sibling(0, k).wait_send()

    for i in range(TILES):
        exchange(0, i).wait_send()

    @pl.loop(1, F)
    def _(j):
        t = lax.rem(f + j, F)
        scatter(t, t, f).wait_send()
        spread(t, f).wait_send()

    @pl.loop(0, F - 1)
    def _(s):
        for d in range(2):
            slot, act = source(d, s)

            @pl.when(act == 1)
            def _():
                for k in range(2):
                    ring(slot, d, k).wait_send()


def per_device(F, hidden, cotangent, down_weight, proj_in, proj_out, valid_proj, lengths):
    T, FFl = hidden.shape
    Dl = cotangent.shape[1]
    H = F // 2
    Tc = T // F
    any_spec = pl.BlockSpec(memory_space=pl.ANY)
    vmem = pl.BlockSpec(memory_space=pltpu.VMEM)
    dma = pltpu.SemaphoreType.DMA
    V = valid_proj.shape[0]
    return pl.pallas_call(
        functools.partial(kernel, F, F == 8),
        out_shape=(
            jax.ShapeDtypeStruct((T, FFl), jnp.bfloat16),
            jax.ShapeDtypeStruct((T // SEQ, V), jnp.float32),
        ),
        in_specs=[pl.BlockSpec(memory_space=pltpu.SMEM)] + [any_spec] * 6,
        out_specs=(any_spec, vmem),
        scratch_shapes=[
            pltpu.VMEM((H, 2, T, Dl), jnp.bfloat16),
            pltpu.VMEM((H, FFl, Dl), jnp.bfloat16),
            pltpu.VMEM((2, T, FFl), jnp.float32),
            pltpu.VMEM((T, FFl), jnp.float32),
            pltpu.VMEM((2, T, FFl // TILES), jnp.bfloat16),
            pltpu.VMEM((T, Dl), jnp.bfloat16),
            pltpu.VMEM((K_OUT, Dl), jnp.bfloat16),
            pltpu.VMEM((FFl, K_IN), jnp.bfloat16),
            pltpu.VMEM((T, K_IN), jnp.float32),
            pltpu.VMEM((F, Tc + Tc // 2, K_IN), jnp.float32),
            pltpu.VMEM((F, Tc + Tc // 2, K_IN), jnp.float32),
            pltpu.VMEM((F, K_OUT, K_IN), jnp.float32),
            pltpu.VMEM((T // SEQ, K_OUT, K_IN), jnp.float32),
            pltpu.VMEM((2, V, CHUNK), jnp.bfloat16),
            dma((5,)), dma((H,)), dma((2,)), dma((2,)), dma((4 * H,)), dma((4 * H,)),
            dma((F,)), dma((F,)), dma((F,)), dma((F,)), dma((TILES,)), dma((TILES,)),
            dma((2,)), dma((2,)),
        ],
        compiler_params=pltpu.CompilerParams(
            collective_id=0, has_side_effects=True, vmem_limit_bytes=66584576
        ),
    )(lengths, hidden, cotangent, down_weight, proj_in, proj_out.T, valid_proj)


def solution(mesh):
    in_specs = (
        P(("group", "dp"), "fsdp"),
        P(("group", "dp"), "fsdp"),
        P("fsdp", "dp"),
        P("fsdp", None),
        P(),
        P(("group", "fsdp"), None),
        P(("group", "dp")),
    )
    out_specs = (P(("group", "dp"), "fsdp"), P(("group", "dp"), "fsdp"))
    return jax.shard_map(
        functools.partial(per_device, mesh.shape["fsdp"]),
        mesh=mesh, in_specs=in_specs, out_specs=out_specs, check_vma=False,
    )
```

```python
import functools

import jax
import jax.numpy as jnp
from jax import lax
from jax.experimental import pallas as pl
from jax.experimental.pallas import tpu as pltpu
from jax.sharding import PartitionSpec as P

K_IN = 128
K_OUT = 64
SEQ = 256
TILES = 7
CHUNK = 1024


def kernel(
    F, snake,
    len_ref, hid, cot, w, pin, pout, vp, out, scores,
    X, W, acc, inc, stage, own, po, pi, act, part, rA, gR, G, vbuf,
    ld_sem, w_sem, sib_send, sib_recv, ring_send, ring_recv,
    rs_send, rs_recv, gs_send, gs_recv, ex_send, ex_recv, out_sem, vp_sem,
):
    f = lax.axis_index("fsdp")
    c = lax.axis_index("dp")
    H = F // 2
    T, Dl = own.shape
    FFl = acc.shape[2]
    Tc = T // F
    tile = FFl // TILES

    if snake:
        y, z = lax.rem(f, 2), f // 2
        p = (1 - y) * z + y * (F - 1 - z)

        def at(q):
            h = q // H
            return (1 - h) * (2 * q) + h * (2 * F - 1 - 2 * q)
    else:
        p = f

        def at(q):
            return q

    targets = (at(lax.rem(p + 1, F)), at(lax.rem(p + F - 1, F)))

    def source(d, s):
        q = lax.rem(p - s + F, F) if d == 0 else lax.rem(p + s, F)
        src = at(q)
        half = src // H
        return src - half * H, 1 - (half + c - 2 * half * c)

    def rows(k):
        return pl.ds(k * SEQ, SEQ)

    def ring(slot, d, k):
        i = slot * 8 + d * 4 + k
        quarter = pl.ds(k * (SEQ // 2), SEQ // 2)
        return pltpu.make_async_remote_copy(
            src_ref=X.at[slot, d, quarter],
            dst_ref=X.at[slot, d, quarter],
            send_sem=ring_send.at[i],
            recv_sem=ring_recv.at[i],
            device_id={"fsdp": targets[d]},
            device_id_type=pl.DeviceIdType.MESH,
        )

    def columns(i):
        return pl.ds(pl.multiple_of(i * tile, tile), tile)

    def exchange(d, i):
        return pltpu.make_async_remote_copy(
            src_ref=acc.at[d, :, columns(i)],
            dst_ref=inc.at[:, columns(i)],
            send_sem=ex_send.at[i],
            recv_sem=ex_recv.at[i],
            device_id={"dp": 1 - c},
            device_id_type=pl.DeviceIdType.MESH,
        )

    my_half = f // H
    my_slot = f - my_half * H

    def sibling(d, k):
        return pltpu.make_async_remote_copy(
            src_ref=own.at[rows(k)],
            dst_ref=X.at[my_slot, d, rows(k)],
            send_sem=sib_send.at[k],
            recv_sem=sib_recv.at[k],
            device_id={"dp": 1 - c},
            device_id_type=pl.DeviceIdType.MESH,
        )

    load_cot = pltpu.make_async_copy(cot, own, ld_sem.at[0])
    load_cot.start()
    load_po = pltpu.make_async_copy(
        pout.at[:, pl.ds(pl.multiple_of(f * Dl, Dl), Dl)], po, ld_sem.at[1]
    )
    load_po.start()
    load_pi = pltpu.make_async_copy(pin, pi, ld_sem.at[2])
    load_pi.start()

    def load_hid(h):
        return pltpu.make_async_copy(
            hid.at[:, pl.ds(h * tile, tile)], stage.at[h % 2], ld_sem.at[3 + h % 2]
        )

    load_hid(0).start()
    load_hid(1).start()

    def load_w(i):
        return pltpu.make_async_copy(w.at[:, pl.ds(i * Dl, Dl)], W.at[i], w_sem.at[i])

    def load_vp(q):
        return pltpu.make_async_copy(
            vp.at[:, pl.ds(q * CHUNK, CHUNK)], vbuf.at[q % 2], vp_sem.at[q % 2]
        )

    barrier = pltpu.get_barrier_semaphore()

    @pl.loop(1, F)
    def _(j):
        pl.semaphore_signal(
            barrier, inc=1, device_id={"fsdp": lax.rem(f + j, F)},
            device_id_type=pl.DeviceIdType.MESH,
        )

    pl.semaphore_signal(
        barrier, inc=1, device_id={"dp": 1 - c}, device_id_type=pl.DeviceIdType.MESH
    )

    load_cot.wait()
    for i in range(H):
        load_w(i).start()
    mine = my_half == c
    for k in range(2):
        position = lax.broadcasted_iota(jnp.int32, (SEQ, Dl), 0)
        block = own[rows(k), :]
        masked = jnp.where(position < len_ref[k], block.astype(jnp.float32), 0.0)
        own[rows(k), :] = masked.astype(block.dtype)
    pl.semaphore_wait(barrier, F)

    @pl.when(my_half != c)
    def _():
        for k in range(2):
            for d in range(2):
                @pl.when(c == d)
                def _():
                    sibling(d, k).start()

    @pl.when(mine)
    def _():
        for k in range(2):
            X[my_slot, c, rows(k), :] = own[rows(k), :]
        for d in range(2):
            @pl.when(c == d)
            def _():
                for k in range(4):
                    ring(my_slot, d, k).start()
        for d in range(2):
            @pl.when(c != d)
            def _():
                for k in range(2):
                    sibling(d, k).wait_recv()
                    ring(my_slot, d, 2 * k).start()
                    ring(my_slot, d, 2 * k + 1).start()

    @pl.loop(0, T // 8)
    def _(i):
        r = pl.ds(pl.multiple_of(i * 8, 8), 8)
        for d in range(2):
            acc[d, r, :] = jnp.zeros((8, FFl), jnp.float32)

    def project_out():
        load_po.wait()
        for k in range(2):
            o = lax.dot_general(
                own[rows(k), :], po[...], (((1,), (1,)), ((), ())),
                preferred_element_type=jnp.float32,
            )
            for j in range(SEQ // Tc):
                first = o[j * Tc : j * Tc + Tc // 2]
                second = o[j * Tc + Tc // 2 : (j + 1) * Tc]
                run = k * (SEQ // Tc) + j
                part[run, Tc : Tc + Tc // 2, 0:K_OUT] = first
                part[run, Tc : Tc + Tc // 2, K_OUT : 2 * K_OUT] = second

    def project_in(start, stop):
        for h in range(start, stop):
            load_hid(h).wait()
            a = jnp.dot(
                stage[h % 2], pi[h * tile : (h + 1) * tile, :],
                preferred_element_type=jnp.float32,
            )
            act[...] = a if h == 0 else act[...] + a
            if h + 2 < TILES:
                load_hid(h + 2).start()

    def scatter(t, src, dst):
        return pltpu.make_async_remote_copy(
            src_ref=part.at[src], dst_ref=rA.at[dst],
            send_sem=rs_send.at[t], recv_sem=rs_recv.at[dst],
            device_id={"fsdp": t}, device_id_type=pl.DeviceIdType.MESH,
        )

    def spread(t, dst):
        return pltpu.make_async_remote_copy(
            src_ref=gR.at[f], dst_ref=gR.at[dst],
            send_sem=gs_send.at[t], recv_sem=gs_recv.at[dst],
            device_id={"fsdp": t}, device_id_type=pl.DeviceIdType.MESH,
        )

    def scatter_acts():
        for j in range(F):
            part[j, 0:Tc, :] = act[j * Tc : (j + 1) * Tc, :]
        for q in range(2):
            load_vp(q).start()

        @pl.loop(1, F)
        def _(j):
            t = lax.rem(f + j, F)
            scatter(t, t, f).start()

    def reduce_acts():
        def add(j, total):
            t = lax.rem(f + j, F)
            scatter(t, t, t).wait_recv()
            return total + rA[t]

        total = lax.fori_loop(1, F, add, part[f])
        tn = (((0,), (0,)), ((), ()))
        g = jnp.zeros((K_OUT, K_IN), jnp.float32)
        for u in range(2):
            g = g + lax.dot_general(
                total[Tc : Tc + Tc // 2, u * K_OUT : (u + 1) * K_OUT],
                total[u * (Tc // 2) : (u + 1) * (Tc // 2), :],
                tn, precision=lax.Precision.HIGHEST,
                preferred_element_type=jnp.float32,
            )
        gR[f] = g

        @pl.loop(1, F)
        def _(j):
            t = lax.rem(f + j, F)
            spread(t, f).start()

    def reduce_grads():
        @pl.loop(1, F)
        def _(j):
            t = lax.rem(f + j, F)
            spread(t, t).wait_recv()

        for e in range(2):
            g = gR[e * H]
            for t in range(1, H):
                g = g + gR[e * H + t]
            G[e] = g
        total = jnp.zeros(scores.shape, jnp.float32)
        for q in range(K_OUT * K_IN // CHUNK):
            load_vp(q).wait()
            per = CHUNK // K_IN
            low = jnp.concatenate(
                [G[:, q * per + u, :] for u in range(per)], axis=1
            ).astype(jnp.bfloat16)
            total = total + lax.dot_general(
                low, vbuf[q % 2], (((1,), (1,)), ((), ())),
                preferred_element_type=jnp.float32,
            )
            if q + 2 < K_OUT * K_IN // CHUNK:
                load_vp(q + 2).start()
        scores[...] = total

    def product(slot, d, last, start=0, stop=TILES):
        @pl.loop(start, stop)
        def _(i):
            n = columns(i)
            acc[d, :, n] += lax.dot_general(
                X[slot, d], W[slot, n, :], (((1,), (1,)), ((), ())),
                preferred_element_type=jnp.float32,
            )

            @pl.when((last == 1) & (c != d))
            def _():
                exchange(d, i).start()

    def forward(s, d, k):
        slot, live = source(d, s)

        @pl.when(live == 1)
        def _():
            ring(slot, d, k).wait_recv()

            @pl.when(s < F - 1)
            def _():
                ring(slot, d, k).start()

    def final(count):
        return 1 - jnp.minimum(H - count, 1)

    def step(s, seen):
        counts = []
        for d in range(2):
            for e in range(2):
                forward(s, e, 2 * d)

            if d == 0:
                @pl.when(s == 1)
                def _():
                    load_pi.wait()
                    project_out()
                    project_in(0, 3)

                @pl.when(s == 2)
                def _():
                    for i in range(H):
                        load_w(i).wait()
            else:
                @pl.when(s == 1)
                def _():
                    project_in(3, TILES)
                    scatter_acts()

            @pl.when((s == 2) & mine)
            def _():
                product(my_slot, d, 0)

            slot, live = source(d, s - 1)
            counts.append(seen[d] + live)

            @pl.when((live == 1) & (s >= 2))
            def _():
                product(slot, d, final(counts[d]), 0, TILES // 2)

            for e in range(2):
                forward(s, e, 2 * d + 1)

            @pl.when((live == 1) & (s >= 2))
            def _():
                product(slot, d, final(counts[d]), TILES // 2, TILES)

        @pl.when(s == 4)
        def _():
            reduce_acts()

        @pl.when(s == 6)
        def _():
            reduce_grads()

        return tuple(counts)

    seen = lax.fori_loop(1, F, step, (0, 0))
    for other in (True, False):
        for d in range(2):
            slot, live = source(d, F - 1)

            @pl.when((live == 1) & ((c != d) if other else (c == d)))
            def _():
                product(slot, d, final(seen[d] + live))

    def write(b):
        return pltpu.make_async_copy(
            stage.at[b % 2], out.at[:, pl.ds(b * tile, tile)], out_sem.at[b % 2]
        )

    for b in range(TILES):
        exchange(0, b).wait_recv()
        if b >= 2:
            write(b - 2).wait()

        @pl.loop(0, T // 16)
        def _(i):
            r = pl.ds(pl.multiple_of(i * 16, 16), 16)
            n = slice(b * tile, (b + 1) * tile)
            stage[b % 2, r, :] = (acc[c, r, n] + inc[r, n]).astype(stage.dtype)

        write(b).start()

    for b in range(TILES - 2, TILES):
        write(b).wait()

    @pl.when(my_half != c)
    def _():
        for k in range(2):
            sibling(0, k).wait_send()

    for i in range(TILES):
        exchange(0, i).wait_send()

    @pl.loop(1, F)
    def _(j):
        t = lax.rem(f + j, F)
        scatter(t, t, f).wait_send()
        spread(t, f).wait_send()

    @pl.loop(0, F - 1)
    def _(s):
        for d in range(2):
            slot, act = source(d, s)

            @pl.when(act == 1)
            def _():
                for k in range(4):
                    ring(slot, d, k).wait_send()


def per_device(F, hidden, cotangent, down_weight, proj_in, proj_out, valid_proj, lengths):
    T, FFl = hidden.shape
    Dl = cotangent.shape[1]
    H = F // 2
    Tc = T // F
    any_spec = pl.BlockSpec(memory_space=pl.ANY)
    vmem = pl.BlockSpec(memory_space=pltpu.VMEM)
    dma = pltpu.SemaphoreType.DMA
    V = valid_proj.shape[0]
    return pl.pallas_call(
        functools.partial(kernel, F, F == 8),
        out_shape=(
            jax.ShapeDtypeStruct((T, FFl), jnp.bfloat16),
            jax.ShapeDtypeStruct((T // SEQ, V), jnp.float32),
        ),
        in_specs=[pl.BlockSpec(memory_space=pltpu.SMEM)] + [any_spec] * 6,
        out_specs=(any_spec, vmem),
        scratch_shapes=[
            pltpu.VMEM((H, 2, T, Dl), jnp.bfloat16),
            pltpu.VMEM((H, FFl, Dl), jnp.bfloat16),
            pltpu.VMEM((2, T, FFl), jnp.float32),
            pltpu.VMEM((T, FFl), jnp.float32),
            pltpu.VMEM((2, T, FFl // TILES), jnp.bfloat16),
            pltpu.VMEM((T, Dl), jnp.bfloat16),
            pltpu.VMEM((K_OUT, Dl), jnp.bfloat16),
            pltpu.VMEM((FFl, K_IN), jnp.bfloat16),
            pltpu.VMEM((T, K_IN), jnp.float32),
            pltpu.VMEM((F, Tc + Tc // 2, K_IN), jnp.float32),
            pltpu.VMEM((F, Tc + Tc // 2, K_IN), jnp.float32),
            pltpu.VMEM((F, K_OUT, K_IN), jnp.float32),
            pltpu.VMEM((T // SEQ, K_OUT, K_IN), jnp.float32),
            pltpu.VMEM((2, V, CHUNK), jnp.bfloat16),
            dma((5,)), dma((H,)), dma((2,)), dma((2,)), dma((8 * H,)), dma((8 * H,)),
            dma((F,)), dma((F,)), dma((F,)), dma((F,)), dma((TILES,)), dma((TILES,)),
            dma((2,)), dma((2,)),
        ],
        compiler_params=pltpu.CompilerParams(
            collective_id=0, has_side_effects=True, vmem_limit_bytes=66584576
        ),
    )(lengths, hidden, cotangent, down_weight, proj_in, proj_out.T, valid_proj)


def solution(mesh):
    in_specs = (
        P(("group", "dp"), "fsdp"),
        P(("group", "dp"), "fsdp"),
        P("fsdp", "dp"),
        P("fsdp", None),
        P(),
        P(("group", "fsdp"), None),
        P(("group", "dp")),
    )
    out_specs = (P(("group", "dp"), "fsdp"), P(("group", "dp"), "fsdp"))
    return jax.shard_map(
        functools.partial(per_device, mesh.shape["fsdp"]),
        mesh=mesh, in_specs=in_specs, out_specs=out_specs, check_vma=False,
    )
```
